32 devices in a mesh: gx: 4 (over y, x), gy: 4 (over z), gz: 2 (over core).
Axes of the slice: x: 2, y: 2, z: 4, core: 2. Of those that a mesh axis runs over, the one named last changes fastest.
Arguments:
- electroneg: float32 [4, 4, 2, 64, 128], P('gx', 'gy', 'gz'), may hold values from 1 to 9
- hardness: float32 [4, 4, 2, 64, 128], P('gx', 'gy', 'gz'), may hold values from 5 to 9
- tiles: float32 [4, 4, 2, 256, 128, 128], P('gx', 'gy', 'gz'), may hold values from -0.19 to 0.19
- pair_rows: int32 [4, 4, 2, 256], P('gx', 'gy', 'gz'), may hold values from 0 to 63
- pair_cols: int32 [4, 4, 2, 256], P('gx', 'gy', 'gz'), may hold values from 0 to 159, as said below
- pair_count: int32 [4, 4, 2], P('gx', 'gy', 'gz'), may hold values from 64 to 256
- ghost_ids: int32 [4, 4, 2, 6, 16], P('gx', 'gy', 'gz'), may hold values from 0 to 63, as said below
Outputs:
- solutions: float32 [2, 4, 4, 2, 64, 128], P(None, 'gx', 'gy', 'gz')
- charges: float32 [4, 4, 2, 64, 128], P('gx', 'gy', 'gz')
The draws below stay inside these ranges and needn't reach their ends.
Inputs may be any that keep to these rules, and one draw needn't show every extreme that they name: `pair_cols`: each slot is a local block (below 64) or a ghost slot. `ghost_ids`: the 16 blocks that a brick sends through one face are distinct.
All inputs are finite; a program needn't handle non-finite values.
Results may differ from the reference program's by a relative error of at most 0.0001.
Values sent between devices are 32-bit elements; how exact they have to be, the bound alone decides.
A program may use at most 64 MiB of HBM per device.

```python
import jax
import jax.numpy as jnp
from jax import lax

ATOMS = 128
NB = 64
GHOST = 16
PAIRS = 256
ITERS = 3
N_GX = 4
N_GY = 4
N_GZ = 2


def slot_columns(key):
    key = jax.random.fold_in(key, 101)
    shape = (N_GX, N_GY, N_GZ, PAIRS)
    pick_key, local_key, ghost_key = jax.random.split(key, 3)
    which = jax.random.randint(pick_key, shape, 0, 3)
    local_slot = jax.random.randint(local_key, shape, 0, NB)
    ghost_slot = NB + jax.random.randint(ghost_key, shape, 0, 6 * GHOST)
    return jnp.where(which < 2, local_slot, ghost_slot).astype(jnp.int32)


def draw_pair_cols(key, part):
    columns = slot_columns(key)
    return columns


def draw_tiles(key, part):
    columns = slot_columns(key)
    key = jax.random.fold_in(key, 13)
    shape = (N_GX, N_GY, N_GZ, PAIRS, ATOMS, ATOMS)
    noise = jnp.clip(0.03 * jax.random.normal(key, shape, jnp.float32), -0.18, 0.18)
    offset = 0.005
    ghost_mark = (columns >= NB).astype(jnp.float32)[..., None, None]
    return (noise + offset * ghost_mark).astype(jnp.float32)


def draw_electroneg(key, part):
    key = jax.random.fold_in(key, 17)
    level_key, atom_key = jax.random.split(key, 2)
    level_shape = (N_GX, N_GY, N_GZ, 1, 1)
    shape = (N_GX, N_GY, N_GZ, NB, ATOMS)
    level = jax.random.uniform(level_key, level_shape, jnp.float32, 2.5, 7.5)
    atom_part = jax.random.uniform(atom_key, shape, jnp.float32, -1.5, 1.5)
    return (level + atom_part).astype(jnp.float32)


def draw_ghost_ids(key, part):
    key = jax.random.fold_in(key, 11)
    count = N_GX * N_GY * N_GZ * 6
    keys = jax.random.split(key, count)
    chosen = jax.vmap(lambda single: jax.random.permutation(single, NB)[:GHOST])(keys)
    return chosen.reshape(N_GX, N_GY, N_GZ, 6, GHOST).astype(jnp.int32)


def set_ends(values, own_key, low, high):
    longest = values.shape.index(max(values.shape))
    spots = []
    for shift in (0, 1):
        where = [jax.random.randint(jax.random.fold_in(own_key, axis), (), 0, length) for axis, length in enumerate(values.shape)]
        where[longest] = (where[longest] + shift) % values.shape[longest]
        spots.append(tuple(where))
    return values.at[spots[0]].set(low).at[spots[1]].set(high)


def block_scale(stream_key, extent, pieces, smallest, high):
    level, own = 1.0, jax.random.fold_in(stream_key, 6)
    for axis_at, blocks in pieces:
        heights = jnp.exp(jax.random.uniform(jax.random.fold_in(own, axis_at), (blocks,), jnp.float32, smallest / len(pieces), high / len(pieces)))
        level = level * jnp.repeat(heights, extent[axis_at] // blocks).reshape([-1 if axis == axis_at else 1 for axis in range(len(extent))])
    return level


def setup_inputs(seed: int = 0) -> dict:
    key_of = jax.random.split(jax.random.key(seed), 8)
    electroneg = draw_electroneg(jax.random.fold_in(key_of[7], 71), 0)
    hardness = jnp.clip(5.0 + 4.0 * jax.random.uniform(key_of[1], (N_GX, N_GY, N_GZ, NB, ATOMS), jnp.float32) ** block_scale(key_of[1], (N_GX, N_GY, N_GZ, NB, ATOMS), ((0, 4), (1, 4), (2, 2)), -0.2, 0.2), 5.0, 9.0)
    tiles = draw_tiles(jax.random.fold_in(key_of[7], 71), 0)
    pair_rows = set_ends(jax.random.randint(key_of[3], (N_GX, N_GY, N_GZ, PAIRS), 0, NB), jax.random.fold_in(key_of[3], 1), 0, NB - 1).astype(jnp.int32)
    pair_cols = draw_pair_cols(jax.random.fold_in(key_of[7], 71), 0)
    pair_count = set_ends(jax.random.randint(key_of[5], (N_GX, N_GY, N_GZ), PAIRS // 4, PAIRS + 1), jax.random.fold_in(key_of[5], 1), PAIRS // 4, PAIRS).astype(jnp.int32)
    ghost_ids = draw_ghost_ids(jax.random.fold_in(key_of[7], 71), 0)
    return dict(electroneg=electroneg, hardness=hardness, tiles=tiles, pair_rows=pair_rows, pair_cols=pair_cols, pair_count=pair_count, ghost_ids=ghost_ids)


def pick(field, ids):
    index = jnp.broadcast_to(ids[None, ..., None], (2,) + ids.shape + (field.shape[-1],)).astype(jnp.int32)
    return jnp.take_along_axis(field, index, axis=4)


def apply_operator(field, hardness, tiles, pair_rows, pair_cols, live, ghost_ids, hot_rows, hot_cols):
    faces = [(1, 1), (1, -1), (2, 1), (2, -1), (3, 1), (3, -1)]
    parts = [field]
    for face, (axis_pos, step) in enumerate(faces):
        parts.append(jnp.roll(pick(field, ghost_ids[:, :, :, face]), step, axis=axis_pos))
    extended = jnp.concatenate(parts, axis=4)
    left = pick(extended, pair_rows)
    right = pick(extended, pair_cols)
    hp = lax.Precision.HIGHEST
    forward = jnp.einsum("xyzpab,sxyzpb->sxyzpa", tiles, right, precision=hp) * live[None, ..., None]
    backward = jnp.einsum("xyzpab,sxyzpa->sxyzpb", tiles, left, precision=hp) * live[None, ..., None]
    slot_sums = jnp.einsum("xyzpk,sxyzpa->sxyzka", hot_rows, forward, precision=hp)
    slot_sums = slot_sums + jnp.einsum("xyzpk,sxyzpa->sxyzka", hot_cols, backward, precision=hp)
    result = hardness[None] * field + slot_sums[:, :, :, :, :NB]
    for face, (axis_pos, step) in enumerate(faces):
        start = NB + face * GHOST
        back = jnp.roll(slot_sums[:, :, :, :, start:start + GHOST], -step, axis=axis_pos)
        hot_ghost = (ghost_ids[:, :, :, face, :, None] == jnp.arange(NB)[None, None, None, None, :]).astype(jnp.float32)
        result = result + jnp.einsum("xyzgk,sxyzga->sxyzka", hot_ghost, back, precision=hp)
    return result


def inner(first, second):
    return jnp.sum(first * second, axis=(1, 2, 3, 4, 5), keepdims=True)


def reference(electroneg, hardness, tiles, pair_rows, pair_cols, pair_count, ghost_ids):
    slots = NB + 6 * GHOST
    live = (jnp.arange(PAIRS)[None, None, None, :] < pair_count[..., None]).astype(jnp.float32)
    hot_rows = (pair_rows[..., None] == jnp.arange(slots)).astype(jnp.float32)
    hot_cols = (pair_cols[..., None] == jnp.arange(slots)).astype(jnp.float32)
    right_side = jnp.stack([-electroneg, -jnp.ones_like(electroneg)])
    solutions = jnp.zeros_like(right_side)
    residual = right_side
    direction = right_side
    norm_now = inner(residual, residual)
    for step in range(ITERS):
        image = apply_operator(direction, hardness, tiles, pair_rows, pair_cols, live, ghost_ids, hot_rows, hot_cols)
        alpha = norm_now / inner(direction, image)
        solutions = solutions + alpha * direction
        residual = residual - alpha * image
        norm_next = inner(residual, residual)
        direction = residual + (norm_next / norm_now) * direction
        norm_now = norm_next
    totals = jnp.sum(solutions, axis=(1, 2, 3, 4, 5))
    charges = solutions[0] - (totals[0] / totals[1]) * solutions[1]
    return solutions, charges
```

```python
import functools

import jax
import jax.numpy as jnp
from jax import lax
from jax.experimental import pallas as pl
from jax.experimental.pallas import tpu as pltpu
from jax.sharding import PartitionSpec as P

ITERS = 3
CHUNKS = 8
F32 = jnp.float32
BF16 = jnp.bfloat16


def split(values):
    high = values.astype(BF16)
    return high, (values - high.astype(F32)).astype(BF16)


def dot(first, second):
    return lax.dot_general(first, second, (((1,), (0,)), ((), ())), preferred_element_type=F32)


def dot_nt(first, second):
    return lax.dot_general(first, second, (((1,), (1,)), ((), ())), preferred_element_type=F32)


def times(hot, parts):
    return dot(hot, parts[0]) + dot(hot, parts[1])


def half_sums(row):
    atoms = row.shape[1] // 2
    sums = [jnp.sum(row[:, s * atoms : (s + 1) * atoms], axis=1, keepdims=True) for s in (0, 1)]
    return jnp.concatenate([jnp.broadcast_to(s, (1, atoms)) for s in sums], axis=1)


def column_sum(values):
    return jnp.sum(values, axis=0, keepdims=True)


def kernel(
    sizes, blocks, ghosts, pairs, atoms,
    count_ref, electroneg_ref, hardness_ref, rows_ref, cols_ref, ghost_ref, tiles_ref,
    solutions_ref, charges_ref,
    raw, tile_high, tile_low, vectors, products, halo_out, halo_in, back_out, back_in,
    part_a, part_b, sum_a, sum_b,
    load_sem, halo_send, halo_recv, back_send, back_recv, a_send, a_recv, b_send, b_recv,
):
    nx, ny, nz = sizes
    ix, iy, iz = lax.axis_index("gx"), lax.axis_index("gy"), lax.axis_index("gz")
    chunk_rows = pairs * atoms // CHUNKS
    loads = []
    for c in range(CHUNKS):
        here = pl.ds(c * chunk_rows, chunk_rows)
        load = pltpu.make_async_copy(tiles_ref.at[here], raw.at[here], load_sem.at[c])
        load.start()
        loads.append(load)

    plane = [
        (lax.rem(ix + ox, nx), iy, lax.rem(iz + oz, nz))
        for ox in range(nx) for oz in range(nz) if ox or oz
    ]
    line = [(ix, lax.rem(iy + oy, ny), iz) for oy in range(1, ny)]
    faces = []
    for axis in range(3):
        for step in (1, -1):
            there, behind = [ix, iy, iz], [ix, iy, iz]
            there[axis] = lax.rem(there[axis] + step + sizes[axis], sizes[axis])
            behind[axis] = lax.rem(behind[axis] - step + sizes[axis], sizes[axis])
            faces.append((tuple(there), tuple(behind)))

    barrier = pltpu.get_barrier_semaphore()
    for peer in plane + line:
        pl.semaphore_signal(barrier, inc=1, device_id=peer, device_id_type=pl.DeviceIdType.MESH)
    pl.semaphore_wait(barrier, len(plane) + len(line))

    def remote(src, dst, send, recv, peer):
        copy = pltpu.make_async_remote_copy(
            src_ref=src, dst_ref=dst, send_sem=send, recv_sem=recv,
            device_id=peer, device_id_type=pl.DeviceIdType.MESH,
        )
        copy.start()
        return copy

    def exchange(out, into, send, recv, it, which):
        copies = []
        for f in range(6):
            here = pl.ds(f * ghosts, ghosts)
            copies.append(remote(
                out.at[it, here], into.at[it, here], send.at[it, f], recv.at[it, f],
                faces[f][which],
            ))
        return copies

    def wait_all(copies):
        for copy in copies:
            copy.wait()

    def gathered_sum(part, arrived, send, recv, it, peers):
        return [
            remote(part.at[it], arrived.at[it, k], send.at[it, k], recv.at[it, k], peer)
            for k, peer in enumerate(peers)
        ]

    def reduce_all(rows, it):
        zeros = jnp.zeros((8 - len(rows), 2 * atoms), F32)
        part_a[it] = jnp.concatenate(rows + [zeros], axis=0)
        wait_all(gathered_sum(part_a, sum_a, a_send, a_recv, it, plane))
        total = part_a[it]
        for k in range(len(plane)):
            total = total + sum_a[it, k]
        part_b[it] = total
        wait_all(gathered_sum(part_b, sum_b, b_send, b_recv, it, line))
        for k in range(len(line)):
            total = total + sum_b[it, k]
        return [half_sums(total[i : i + 1]) for i in range(len(rows))]

    slots = 2 * atoms
    live = lax.broadcasted_iota(jnp.int32, (slots, pairs), 1) < count_ref[0, 0]
    slot_of = lax.broadcasted_iota(jnp.int32, (slots, pairs), 0)
    hot_rows = jnp.where((slot_of == rows_ref[...]) & live, 1.0, 0.0)
    hot_cols = jnp.where((slot_of == cols_ref[...]) & live, 1.0, 0.0)
    hot_ghost = jnp.where(
        lax.broadcasted_iota(jnp.int32, (atoms, atoms), 0) == ghost_ref[...], 1.0, 0.0
    )
    pick_rows = jnp.transpose(hot_rows)[:, :atoms].astype(BF16)
    pick_cols = jnp.transpose(hot_cols).astype(BF16)
    pick_ghost = jnp.transpose(hot_ghost).astype(BF16)
    hot_rows = hot_rows[:blocks].astype(BF16)
    hot_cols = hot_cols[: blocks + 6 * ghosts].astype(BF16)
    hot_ghost = hot_ghost[:blocks].astype(BF16)
    pad_rows = jnp.zeros((atoms - blocks, 2 * atoms), F32)
    pad_slots = jnp.zeros((slots - blocks - 6 * ghosts, 2 * atoms), F32)
    pad_ghost = jnp.zeros((atoms - 6 * ghosts, 2 * atoms), F32)

    row8 = lax.broadcasted_iota(jnp.int32, (8, atoms), 0)
    keep_high = jnp.where(row8 % 4 < 2, 1.0, 0.0)
    first_pair = row8 < 4

    def put_vectors(high, low):
        for k, part in enumerate((high, low)):
            vectors[pl.ds(2 * k, pairs, stride=4), :] = part[:, :atoms]
            vectors[pl.ds(2 * k + 1, pairs, stride=4), :] = part[:, atoms:]

    def take_products():
        first = [products[pl.ds(k, pairs, stride=4), :] for k in range(4)]
        return jnp.concatenate([first[0] + first[2], first[1] + first[3]], axis=1)

    def tile_loop(backward):
        def step(i, carry):
            at = pl.ds(pl.multiple_of(i * 8, 8), 8)
            here = pl.ds(pl.multiple_of(i * 2 * atoms, 2 * atoms), 2 * atoms)
            both = vectors[at, :]
            all_parts = both.astype(BF16)
            high_part = (both * keep_high).astype(BF16)
            high, low = tile_high[here, :], tile_low[here, :]
            if backward:
                lhs = jnp.concatenate([all_parts, high_part], axis=1)
                pair = [
                    jnp.concatenate([high[s * atoms : (s + 1) * atoms], low[s * atoms : (s + 1) * atoms]], axis=0)
                    for s in (0, 1)
                ]
                out = dot(lhs, jnp.concatenate(pair, axis=1))
            else:
                out = dot_nt(all_parts, high) + dot_nt(high_part, low)
            products[at, :] = jnp.where(first_pair, out[:, :atoms], out[:, atoms:])
            return carry

        lax.fori_loop(0, pairs // 2, step, 0, unroll=8)

    hardness = hardness_ref[...]
    hardness = jnp.concatenate([hardness, hardness], axis=1)
    electroneg = electroneg_ref[...]
    residual = jnp.concatenate([-electroneg, -jnp.ones_like(electroneg)], axis=1)
    direction = residual
    solutions = jnp.zeros_like(residual)

    for it in range(ITERS):
        last = it == ITERS - 1
        parts = split(jnp.concatenate([direction, pad_rows], axis=0))
        halo_out[it] = times(pick_ghost, parts)[: 6 * ghosts]
        halo_copies = exchange(halo_out, halo_in, halo_send, halo_recv, it, 0)
        put_vectors(dot(pick_rows, parts[0]), dot(pick_rows, parts[1]))
        if it == 0:
            for c in range(CHUNKS):
                loads[c].wait()

                def convert(i, carry, c=c):
                    here = pl.ds(pl.multiple_of(c * chunk_rows + i * 256, 256), 256)
                    high, low = split(raw[here, :])
                    tile_high[here, :] = high
                    tile_low[here, :] = low
                    return carry

                lax.fori_loop(0, chunk_rows // 256, convert, 0)
        tile_loop(True)
        backward = take_products()
        if not last:
            sums = times(hot_cols, split(backward))
            back_out[it] = sums[blocks:]
            back_copies = exchange(back_out, back_in, back_send, back_recv, it, 1)
        wait_all(halo_copies)
        extended = split(jnp.concatenate([direction, halo_in[it], pad_slots], axis=0))
        right_high, right_low = dot(pick_cols, extended[0]), dot(pick_cols, extended[1])
        if last:
            curve = column_sum(hardness * direction * direction)
            curve = curve + 2.0 * column_sum(backward * (right_high + right_low))
            norm, curve, total_x, total_d = reduce_all(
                [column_sum(residual * residual), curve, column_sum(solutions), column_sum(direction)], it
            )
            alpha = norm / curve
            solutions = solutions + alpha * direction
            totals = total_x + alpha * total_d
            ratio = totals[:, :atoms] / totals[:, atoms:]
            solutions_ref[0] = solutions[:, :atoms]
            solutions_ref[1] = solutions[:, atoms:]
            charges_ref[...] = solutions[:, :atoms] - ratio * solutions[:, atoms:]
        else:
            put_vectors(right_high, right_low)
            tile_loop(False)
            forward = take_products()
            own = sums[:blocks] + times(hot_rows, split(forward))
            wait_all(back_copies)
            returned = split(jnp.concatenate([back_in[it], pad_ghost], axis=0))
            image = hardness * direction + own + times(hot_ghost, returned)
            norm, curve, cross, square = reduce_all(
                [
                    column_sum(residual * residual), column_sum(direction * image),
                    column_sum(residual * image), column_sum(image * image),
                ], it
            )
            alpha = norm / curve
            solutions = solutions + alpha * direction
            residual = residual - alpha * image
            beta = (norm - 2.0 * alpha * cross + alpha * alpha * square) / norm
            direction = residual + beta * direction


def body(electroneg, hardness, tiles, pair_rows, pair_cols, pair_count, ghost_ids):
    sizes = tuple(lax.axis_size(name) for name in ("gx", "gy", "gz"))
    blocks, atoms = electroneg.shape[3:]
    pairs = tiles.shape[3]
    ghosts = ghost_ids.shape[4]
    ghost_row = jnp.pad(
        ghost_ids.reshape(1, 6 * ghosts), ((0, 0), (0, atoms - 6 * ghosts)), constant_values=-1
    )
    in_plane, in_line = sizes[0] * sizes[2] - 1, sizes[1] - 1
    vmem = pl.BlockSpec(memory_space=pltpu.VMEM)
    wide = 2 * atoms
    dma = pltpu.SemaphoreType.DMA
    solutions, charges = pl.pallas_call(
        functools.partial(kernel, sizes, blocks, ghosts, pairs, atoms),
        out_shape=(
            jax.ShapeDtypeStruct((2, blocks, atoms), F32),
            jax.ShapeDtypeStruct((blocks, atoms), F32),
        ),
        in_specs=[pl.BlockSpec(memory_space=pltpu.SMEM)] + [vmem] * 5 + [pl.BlockSpec(memory_space=pl.ANY)],
        out_specs=(vmem, vmem),
        scratch_shapes=[
            pltpu.VMEM((pairs * atoms, atoms), F32),
            pltpu.VMEM((pairs * atoms, atoms), BF16),
            pltpu.VMEM((pairs * atoms, atoms), BF16),
            pltpu.VMEM((pairs * 4, atoms), F32),
            pltpu.VMEM((pairs * 4, atoms), F32),
            pltpu.VMEM((ITERS, 6 * ghosts, wide), F32),
            pltpu.VMEM((ITERS, 6 * ghosts, wide), F32),
            pltpu.VMEM((ITERS - 1, 6 * ghosts, wide), F32),
            pltpu.VMEM((ITERS - 1, 6 * ghosts, wide), F32),
            pltpu.VMEM((ITERS, 8, wide), F32),
            pltpu.VMEM((ITERS, 8, wide), F32),
            pltpu.VMEM((ITERS, in_plane, 8, wide), F32),
            pltpu.VMEM((ITERS, in_line, 8, wide), F32),
            dma((CHUNKS,)),
            dma((ITERS, 6)), dma((ITERS, 6)),
            dma((ITERS - 1, 6)), dma((ITERS - 1, 6)),
            dma((ITERS, in_plane)), dma((ITERS, in_plane)),
            dma((ITERS, in_line)), dma((ITERS, in_line)),
        ],
        compiler_params=pltpu.CompilerParams(
            collective_id=0, has_side_effects=True, vmem_limit_bytes=48 * 1024 * 1024
        ),
    )(
        pair_count.reshape(1, 1),
        electroneg.reshape(blocks, atoms),
        hardness.reshape(blocks, atoms),
        pair_rows.reshape(1, pairs),
        pair_cols.reshape(1, pairs),
        ghost_row,
        tiles.reshape(pairs * atoms, atoms),
    )
    return solutions.reshape((2, 1, 1, 1, blocks, atoms)), charges.reshape((1, 1, 1, blocks, atoms))


def solution(mesh):
    return jax.shard_map(
        body,
        mesh=mesh,
        in_specs=(
            P("gx", "gy", "gz", None, None),
            P("gx", "gy", "gz", None, None),
            P("gx", "gy", "gz", None, None, None),
            P("gx", "gy", "gz", None),
            P("gx", "gy", "gz", None),
            P("gx", "gy", "gz"),
            P("gx", "gy", "gz", None, None),
        ),
        out_specs=(P(None, "gx", "gy", "gz", None, None), P("gx", "gy", "gz", None, None)),
        check_vma=False,
    )
```

```python
import functools
import math

import jax
import jax.numpy as jnp
from jax import lax
from jax.experimental import pallas as pl
from jax.experimental.pallas import tpu as pltpu
from jax.sharding import PartitionSpec as P

ITERS = 3
CHUNKS = 8
UNROLL = 32
DIRECT = 32
F32 = jnp.float32
BF16 = jnp.bfloat16


def split(values):
    high = values.astype(BF16)
    return high, (values - high.astype(F32)).astype(BF16)


def dot(first, second):
    return lax.dot_general(first, second, (((1,), (0,)), ((), ())), preferred_element_type=F32)


def dot_nt(first, second):
    return lax.dot_general(first, second, (((1,), (1,)), ((), ())), preferred_element_type=F32)


def times(hot, parts):
    return dot(hot, parts[0]) + dot(hot, parts[1])


def column_sum(values):
    return jnp.sum(values, axis=0, keepdims=True)


def kernel(
    sizes, spreads, blocks, ghosts, pairs, atoms,
    count_ref, electroneg_ref, hardness_ref, rows_ref, cols_ref, ghost_ref, tiles_ref,
    solutions_ref, charges_ref,
    raw, tile_high, tile_low, vectors, products, halo_out, halo_in, back_out, back_in,
    load_sem, halo_send, halo_recv, back_send, back_recv, *reduce_refs,
):
    nx, ny, nz = sizes
    stages = len(spreads)
    reducers = [reduce_refs[k * stages : (k + 1) * stages] for k in range(4)]
    ix, iy, iz = lax.axis_index("gx"), lax.axis_index("gy"), lax.axis_index("gz")
    chunk_rows = pairs * atoms // CHUNKS
    loads = []
    for c in range(CHUNKS):
        here = pl.ds(c * chunk_rows, chunk_rows)
        load = pltpu.make_async_copy(tiles_ref.at[here], raw.at[here], load_sem.at[c])
        load.start()
        loads.append(load)

    def group_of(spread):
        offsets = [(ox, oy, oz) for ox in range(spread[0]) for oy in range(spread[1]) for oz in range(spread[2])]
        return [
            (lax.rem(ix + ox, nx), lax.rem(iy + oy, ny), lax.rem(iz + oz, nz)) for ox, oy, oz in offsets[1:]
        ]

    groups = [group_of(spread) for spread in spreads]
    faces = []
    for axis in range(3):
        for step in (1, -1):
            there, behind = [ix, iy, iz], [ix, iy, iz]
            there[axis] = lax.rem(there[axis] + step + sizes[axis], sizes[axis])
            behind[axis] = lax.rem(behind[axis] - step + sizes[axis], sizes[axis])
            faces.append((tuple(there), tuple(behind)))

    barrier = pltpu.get_barrier_semaphore()
    for peer in sum(groups, []):
        pl.semaphore_signal(barrier, inc=1, device_id=peer, device_id_type=pl.DeviceIdType.MESH)

    def remote(src, dst, send, recv, peer):
        copy = pltpu.make_async_remote_copy(
            src_ref=src, dst_ref=dst, send_sem=send, recv_sem=recv,
            device_id=peer, device_id_type=pl.DeviceIdType.MESH,
        )
        copy.start()
        return copy

    def exchange(out, into, send, recv, it, which):
        copies = []
        for f in range(6):
            here = pl.ds(f * ghosts, ghosts)
            copies.append(remote(
                out.at[it, here], into.at[it, here], send.at[it, f], recv.at[it, f],
                faces[f][which],
            ))
        return copies

    def wait_all(copies):
        for copy in copies:
            copy.wait()

    def gathered_sum(part, arrived, send, recv, it, peers):
        return [
            remote(part.at[it], arrived.at[it, k], send.at[it, k], recv.at[it, k], peer)
            for k, peer in enumerate(peers)
        ]

    def reduce_all(rows, it):
        total = jnp.concatenate([row[:, :atoms] for row in rows] + [row[:, atoms:] for row in rows], axis=0)
        for group, part, arrived, send, recv in zip(groups, *reducers):
            part[it] = total
            wait_all(gathered_sum(part, arrived, send, recv, it, group))
            for k in range(len(group)):
                total = total + arrived[it, k]
        sums = jnp.broadcast_to(jnp.sum(total, axis=1, keepdims=True), total.shape)
        n = len(rows)
        return [jnp.concatenate([sums[i : i + 1], sums[n + i : n + i + 1]], axis=1) for i in range(n)]

    slots = 2 * atoms
    live = lax.broadcasted_iota(jnp.int32, (slots, pairs), 1) < count_ref[0, 0]
    slot_of = lax.broadcasted_iota(jnp.int32, (slots, pairs), 0)
    hot_rows = jnp.where((slot_of == rows_ref[...]) & live, 1.0, 0.0)
    hot_cols = jnp.where((slot_of == cols_ref[...]) & live, 1.0, 0.0)
    hot_ghost = jnp.where(
        lax.broadcasted_iota(jnp.int32, (atoms, atoms), 0) == ghost_ref[...], 1.0, 0.0
    )
    pick_rows = jnp.transpose(hot_rows)[:, :atoms].astype(BF16)
    pick_cols = jnp.transpose(hot_cols).astype(BF16)
    pick_ghost = jnp.transpose(hot_ghost).astype(BF16)
    hot_rows = hot_rows[:blocks].astype(BF16)
    hot_cols = hot_cols[: blocks + 6 * ghosts].astype(BF16)
    hot_ghost = hot_ghost[:blocks].astype(BF16)
    pad_rows = jnp.zeros((atoms - blocks, 2 * atoms), F32)
    pad_slots = jnp.zeros((slots - blocks - 6 * ghosts, 2 * atoms), F32)
    pad_ghost = jnp.zeros((atoms - 6 * ghosts, 2 * atoms), F32)

    row8 = lax.broadcasted_iota(jnp.int32, (8, atoms), 0)
    keep_high = jnp.where(row8 % 4 < 2, 1.0, 0.0)
    first_pair = row8 < 4

    def put_vectors(high, low):
        for k, part in enumerate((high, low)):
            vectors[pl.ds(2 * k, pairs, stride=4), :] = part[:, :atoms]
            vectors[pl.ds(2 * k + 1, pairs, stride=4), :] = part[:, atoms:]

    def take_products():
        first = [products[pl.ds(k, pairs, stride=4), :] for k in range(4)]
        return jnp.concatenate([first[0] + first[2], first[1] + first[3]], axis=1)

    def tile_loop(backward, start, stop):
        def step(i, carry):
            at = pl.ds(pl.multiple_of(i * 8, 8), 8)
            here = pl.ds(pl.multiple_of(i * 2 * atoms, 2 * atoms), 2 * atoms)
            both = vectors[at, :]
            all_parts = both.astype(BF16)
            high_part = (both * keep_high).astype(BF16)
            high, low = tile_high[here, :], tile_low[here, :]
            if backward:
                lhs = jnp.concatenate([all_parts, high_part], axis=1)
                pair = [
                    jnp.concatenate([high[s * atoms : (s + 1) * atoms], low[s * atoms : (s + 1) * atoms]], axis=0)
                    for s in (0, 1)
                ]
                out = dot(lhs, jnp.concatenate(pair, axis=1))
            else:
                out = dot_nt(all_parts, high) + dot_nt(high_part, low)
            products[at, :] = jnp.where(first_pair, out[:, :atoms], out[:, atoms:])
            return carry

        lax.fori_loop(start, stop, step, 0, unroll=min(UNROLL, stop - start))

    pl.semaphore_wait(barrier, sum(len(group) for group in groups))

    hardness = hardness_ref[...]
    hardness = jnp.concatenate([hardness, hardness], axis=1)
    electroneg = electroneg_ref[...]
    residual = jnp.concatenate([-electroneg, -jnp.ones_like(electroneg)], axis=1)
    direction = residual
    solutions = jnp.zeros_like(residual)

    for it in range(ITERS):
        last = it == ITERS - 1
        parts = split(jnp.concatenate([direction, pad_rows], axis=0))
        halo_out[it] = times(pick_ghost, parts)[: 6 * ghosts]
        halo_copies = exchange(halo_out, halo_in, halo_send, halo_recv, it, 0)
        put_vectors(dot(pick_rows, parts[0]), dot(pick_rows, parts[1]))
        if it == 0:
            for c in range(CHUNKS):
                loads[c].wait()

                def convert(i, carry, c=c):
                    here = pl.ds(pl.multiple_of(c * chunk_rows + i * 256, 256), 256)
                    high, low = split(raw[here, :])
                    tile_high[here, :] = high
                    tile_low[here, :] = low
                    return carry

                lax.fori_loop(0, chunk_rows // 256, convert, 0)
                tile_loop(True, c * pairs // (2 * CHUNKS), (c + 1) * pairs // (2 * CHUNKS))
        else:
            tile_loop(True, 0, pairs // 2)
        backward = take_products()
        if not last:
            sums = times(hot_cols, split(backward))
            back_out[it] = sums[blocks:]
            back_copies = exchange(back_out, back_in, back_send, back_recv, it, 1)
        wait_all(halo_copies)
        extended = split(jnp.concatenate([direction, halo_in[it], pad_slots], axis=0))
        right_high, right_low = dot(pick_cols, extended[0]), dot(pick_cols, extended[1])
        if last:
            curve = column_sum(hardness * direction * direction)
            curve = curve + 2.0 * column_sum(backward * (right_high + right_low))
            norm, curve, total_x, total_d = reduce_all(
                [column_sum(residual * residual), curve, column_sum(solutions), column_sum(direction)], it
            )
            alpha = norm / curve
            solutions = solutions + alpha * direction
            totals = total_x + alpha * total_d
            ratio = totals[:, :atoms] / totals[:, atoms:]
            solutions_ref[0] = solutions[:, :atoms]
            solutions_ref[1] = solutions[:, atoms:]
            charges_ref[...] = solutions[:, :atoms] - ratio * solutions[:, atoms:]
        else:
            put_vectors(right_high, right_low)
            tile_loop(False, 0, pairs // 2)
            forward = take_products()
            own = sums[:blocks] + times(hot_rows, split(forward))
            wait_all(back_copies)
            returned = split(jnp.concatenate([back_in[it], pad_ghost], axis=0))
            image = hardness * direction + own + times(hot_ghost, returned)
            norm, curve, cross, square = reduce_all(
                [
                    column_sum(residual * residual), column_sum(direction * image),
                    column_sum(residual * image), column_sum(image * image),
                ], it
            )
            alpha = norm / curve
            solutions = solutions + alpha * direction
            residual = residual - alpha * image
            beta = (norm - 2.0 * alpha * cross + alpha * alpha * square) / norm
            direction = residual + beta * direction


def body(electroneg, hardness, tiles, pair_rows, pair_cols, pair_count, ghost_ids):
    sizes = tuple(lax.axis_size(name) for name in ("gx", "gy", "gz"))
    blocks, atoms = electroneg.shape[3:]
    pairs = tiles.shape[3]
    ghosts = ghost_ids.shape[4]
    ghost_row = jnp.pad(
        ghost_ids.reshape(1, 6 * ghosts), ((0, 0), (0, atoms - 6 * ghosts)), constant_values=-1
    )
    spreads = [sizes] if math.prod(sizes) <= DIRECT else [(sizes[0], 1, sizes[2]), (1, sizes[1], 1)]
    peers = [math.prod(spread) - 1 for spread in spreads]
    vmem = pl.BlockSpec(memory_space=pltpu.VMEM)
    wide = 2 * atoms
    dma = pltpu.SemaphoreType.DMA
    solutions, charges = pl.pallas_call(
        functools.partial(kernel, sizes, spreads, blocks, ghosts, pairs, atoms),
        out_shape=(
            jax.ShapeDtypeStruct((2, blocks, atoms), F32),
            jax.ShapeDtypeStruct((blocks, atoms), F32),
        ),
        in_specs=[pl.BlockSpec(memory_space=pltpu.SMEM)] + [vmem] * 5 + [pl.BlockSpec(memory_space=pl.ANY)],
        out_specs=(vmem, vmem),
        scratch_shapes=[
            pltpu.VMEM((pairs * atoms, atoms), F32),
            pltpu.VMEM((pairs * atoms, atoms), BF16),
            pltpu.VMEM((pairs * atoms, atoms), BF16),
            pltpu.VMEM((pairs * 4, atoms), F32),
            pltpu.VMEM((pairs * 4, atoms), F32),
            pltpu.VMEM((ITERS, 6 * ghosts, wide), F32),
            pltpu.VMEM((ITERS, 6 * ghosts, wide), F32),
            pltpu.VMEM((ITERS - 1, 6 * ghosts, wide), F32),
            pltpu.VMEM((ITERS - 1, 6 * ghosts, wide), F32),
            dma((CHUNKS,)),
            dma((ITERS, 6)), dma((ITERS, 6)),
            dma((ITERS - 1, 6)), dma((ITERS - 1, 6)),
            *[pltpu.VMEM((ITERS, 8, atoms), F32) for _ in peers],
            *[pltpu.VMEM((ITERS, n, 8, atoms), F32) for n in peers],
            *[dma((ITERS, n)) for n in peers],
            *[dma((ITERS, n)) for n in peers],
        ],
        compiler_params=pltpu.CompilerParams(
            collective_id=0, has_side_effects=True, vmem_limit_bytes=48 * 1024 * 1024
        ),
    )(
        pair_count.reshape(1, 1),
        electroneg.reshape(blocks, atoms),
        hardness.reshape(blocks, atoms),
        pair_rows.reshape(1, pairs),
        pair_cols.reshape(1, pairs),
        ghost_row,
        tiles.reshape(pairs * atoms, atoms),
    )
    return solutions.reshape((2, 1, 1, 1, blocks, atoms)), charges.reshape((1, 1, 1, blocks, atoms))


def solution(mesh):
    return jax.shard_map(
        body,
        mesh=mesh,
        in_specs=(
            P("gx", "gy", "gz", None, None),
            P("gx", "gy", "gz", None, None),
            P("gx", "gy", "gz", None, None, None),
            P("gx", "gy", "gz", None),
            P("gx", "gy", "gz", None),
            P("gx", "gy", "gz"),
            P("gx", "gy", "gz", None, None),
        ),
        out_specs=(P(None, "gx", "gy", "gz", None, None), P("gx", "gy", "gz", None, None)),
        check_vma=False,
    )
```

```python
import functools
import math

import jax
import jax.numpy as jnp
from jax import lax
from jax.experimental import pallas as pl
from jax.experimental.pallas import tpu as pltpu
from jax.sharding import PartitionSpec as P

ITERS = 3
CHUNKS = 8
UNROLL = 64
DIRECT = 32
F32 = jnp.float32
BF16 = jnp.bfloat16


def split(values):
    high = values.astype(BF16)
    return high, (values - high.astype(F32)).astype(BF16)


def dot(first, second):
    return lax.dot_general(first, second, (((1,), (0,)), ((), ())), preferred_element_type=F32)


def dot_nt(first, second):
    return lax.dot_general(first, second, (((1,), (1,)), ((), ())), preferred_element_type=F32)


def times(hot, parts):
    return dot(hot, parts[0]) + dot(hot, parts[1])


def column_sum(values):
    return jnp.sum(values, axis=0, keepdims=True)


def kernel(
    sizes, spreads, blocks, ghosts, pairs, atoms,
    count_ref, electroneg_ref, hardness_ref, rows_ref, cols_ref, ghost_ref, tiles_ref,
    solutions_ref, charges_ref,
    raw, tile_high, tile_low, vectors, products, halo_out, halo_in, back_out, back_in,
    load_sem, halo_send, halo_recv, back_send, back_recv, *reduce_refs,
):
    nx, ny, nz = sizes
    stages = len(spreads)
    reducers = [reduce_refs[k * stages : (k + 1) * stages] for k in range(4)]
    ix, iy, iz = lax.axis_index("gx"), lax.axis_index("gy"), lax.axis_index("gz")
    chunk_rows = pairs * atoms // CHUNKS
    loads = []
    for c in range(CHUNKS):
        here = pl.ds(c * chunk_rows, chunk_rows)
        load = pltpu.make_async_copy(tiles_ref.at[here], raw.at[here], load_sem.at[c])
        load.start()
        loads.append(load)

    def group_of(spread):
        offsets = [(ox, oy, oz) for ox in range(spread[0]) for oy in range(spread[1]) for oz in range(spread[2])]
        return [
            (lax.rem(ix + ox, nx), lax.rem(iy + oy, ny), lax.rem(iz + oz, nz)) for ox, oy, oz in offsets[1:]
        ]

    groups = [group_of(spread) for spread in spreads]
    faces = []
    for axis in range(3):
        for step in (1, -1):
            there, behind = [ix, iy, iz], [ix, iy, iz]
            there[axis] = lax.rem(there[axis] + step + sizes[axis], sizes[axis])
            behind[axis] = lax.rem(behind[axis] - step + sizes[axis], sizes[axis])
            faces.append((tuple(there), tuple(behind)))

    barrier = pltpu.get_barrier_semaphore()
    for peer in sum(groups, []):
        pl.semaphore_signal(barrier, inc=1, device_id=peer, device_id_type=pl.DeviceIdType.MESH)

    def remote(src, dst, send, recv, peer):
        copy = pltpu.make_async_remote_copy(
            src_ref=src, dst_ref=dst, send_sem=send, recv_sem=recv,
            device_id=peer, device_id_type=pl.DeviceIdType.MESH,
        )
        copy.start()
        return copy

    def exchange(out, into, send, recv, it, which):
        copies = []
        for f in range(6):
            here = pl.ds(f * ghosts, ghosts)
            copies.append(remote(
                out.at[it, here], into.at[it, here], send.at[it, f], recv.at[it, f],
                faces[f][which],
            ))
        return copies

    departures = []

    def wait_all(copies):
        departures.extend(copies)
        for copy in copies:
            copy.wait_recv()

    def gathered_sum(part, arrived, send, recv, it, peers):
        return [
            remote(part.at[it], arrived.at[it, k], send.at[it, k], recv.at[it, k], peer)
            for k, peer in enumerate(peers)
        ]

    def reduce_all(rows, it):
        total = jnp.concatenate([row[:, :atoms] for row in rows] + [row[:, atoms:] for row in rows], axis=0)
        for group, part, arrived, send, recv in zip(groups, *reducers):
            part[it] = total
            copies = gathered_sum(part, arrived, send, recv, it, group)
            departures.extend(copies)
            for copy in copies:
                copy.wait_recv()
            for k in range(len(group)):
                total = total + arrived[it, k]
        sums = jnp.broadcast_to(jnp.sum(total, axis=1, keepdims=True), total.shape)
        n = len(rows)
        return [jnp.concatenate([sums[i : i + 1], sums[n + i : n + i + 1]], axis=1) for i in range(n)]

    slots = 2 * atoms
    live = lax.broadcasted_iota(jnp.int32, (slots, pairs), 1) < count_ref[0, 0]
    slot_of = lax.broadcasted_iota(jnp.int32, (slots, pairs), 0)
    hot_rows = jnp.where((slot_of == rows_ref[...]) & live, 1.0, 0.0)
    hot_cols = jnp.where((slot_of == cols_ref[...]) & live, 1.0, 0.0)
    hot_ghost = jnp.where(
        lax.broadcasted_iota(jnp.int32, (atoms, atoms), 0) == ghost_ref[...], 1.0, 0.0
    )
    pick_rows = jnp.transpose(hot_rows)[:, :atoms].astype(BF16)
    pick_cols = jnp.transpose(hot_cols).astype(BF16)
    pick_ghost = jnp.transpose(hot_ghost).astype(BF16)
    hot_rows = hot_rows[:blocks].astype(BF16)
    hot_cols = hot_cols[: blocks + 6 * ghosts].astype(BF16)
    hot_ghost = hot_ghost[:blocks].astype(BF16)
    pad_rows = jnp.zeros((atoms - blocks, 2 * atoms), F32)
    pad_slots = jnp.zeros((slots - blocks - 6 * ghosts, 2 * atoms), F32)
    pad_ghost = jnp.zeros((atoms - 6 * ghosts, 2 * atoms), F32)

    row8 = lax.broadcasted_iota(jnp.int32, (8, atoms), 0)
    keep_high = jnp.where(row8 % 4 < 2, 1.0, 0.0)
    first_pair = row8 < 4

    def put_vectors(high, low):
        for k, part in enumerate((high, low)):
            vectors[pl.ds(2 * k, pairs, stride=4), :] = part[:, :atoms]
            vectors[pl.ds(2 * k + 1, pairs, stride=4), :] = part[:, atoms:]

    def take_products():
        first = [products[pl.ds(k, pairs, stride=4), :] for k in range(4)]
        return jnp.concatenate([first[0] + first[2], first[1] + first[3]], axis=1)

    def tile_loop(backward, start, stop):
        def step(i, carry):
            at = pl.ds(pl.multiple_of(i * 8, 8), 8)
            here = pl.ds(pl.multiple_of(i * 2 * atoms, 2 * atoms), 2 * atoms)
            both = vectors[at, :]
            all_parts = both.astype(BF16)
            high_part = (both * keep_high).astype(BF16)
            high, low = tile_high[here, :], tile_low[here, :]
            if backward:
                lhs = jnp.concatenate([all_parts, high_part], axis=1)
                pair = [
                    jnp.concatenate([high[s * atoms : (s + 1) * atoms], low[s * atoms : (s + 1) * atoms]], axis=0)
                    for s in (0, 1)
                ]
                out = dot(lhs, jnp.concatenate(pair, axis=1))
            else:
                out = dot_nt(jnp.concatenate([all_parts, high_part], axis=1), jnp.concatenate([high, low], axis=1))
            products[at, :] = jnp.where(first_pair, out[:, :atoms], out[:, atoms:])
            return carry

        lax.fori_loop(start, stop, step, 0, unroll=min(UNROLL, stop - start))

    pl.semaphore_wait(barrier, sum(len(group) for group in groups))

    hardness = hardness_ref[...]
    hardness = jnp.concatenate([hardness, hardness], axis=1)
    electroneg = electroneg_ref[...]
    residual = jnp.concatenate([-electroneg, -jnp.ones_like(electroneg)], axis=1)
    direction = residual
    solutions = jnp.zeros_like(residual)

    for it in range(ITERS):
        last = it == ITERS - 1
        parts = split(jnp.concatenate([direction, pad_rows], axis=0))
        halo_out[it] = times(pick_ghost, parts)[: 6 * ghosts]
        halo_copies = exchange(halo_out, halo_in, halo_send, halo_recv, it, 0)
        put_vectors(dot(pick_rows, parts[0]), dot(pick_rows, parts[1]))
        if it == 0:
            for c in range(CHUNKS):
                loads[c].wait()

                def convert(i, carry, c=c):
                    here = pl.ds(pl.multiple_of(c * chunk_rows + i * 256, 256), 256)
                    high, low = split(raw[here, :])
                    tile_high[here, :] = high
                    tile_low[here, :] = low
                    return carry

                lax.fori_loop(0, chunk_rows // 256, convert, 0)
                tile_loop(True, c * pairs // (2 * CHUNKS), (c + 1) * pairs // (2 * CHUNKS))
        else:
            tile_loop(True, 0, pairs // 2)
        backward = take_products()
        if not last:
            sums = times(hot_cols, split(backward))
            back_out[it] = sums[blocks:]
            back_copies = exchange(back_out, back_in, back_send, back_recv, it, 1)
        wait_all(halo_copies)
        extended = split(jnp.concatenate([direction, halo_in[it], pad_slots], axis=0))
        right_high, right_low = dot(pick_cols, extended[0]), dot(pick_cols, extended[1])
        if last:
            curve = column_sum(hardness * direction * direction)
            curve = curve + 2.0 * column_sum(backward * (right_high + right_low))
            norm, curve, total_x, total_d = reduce_all(
                [column_sum(residual * residual), curve, column_sum(solutions), column_sum(direction)], it
            )
            alpha = norm / curve
            solutions = solutions + alpha * direction
            totals = total_x + alpha * total_d
            ratio = totals[:, :atoms] / totals[:, atoms:]
            solutions_ref[0] = solutions[:, :atoms]
            solutions_ref[1] = solutions[:, atoms:]
            charges_ref[...] = solutions[:, :atoms] - ratio * solutions[:, atoms:]
            for copy in departures:
                copy.wait_send()
        else:
            put_vectors(right_high, right_low)
            tile_loop(False, 0, pairs // 2)
            forward = take_products()
            own = sums[:blocks] + times(hot_rows, split(forward))
            wait_all(back_copies)
            returned = split(jnp.concatenate([back_in[it], pad_ghost], axis=0))
            image = hardness * direction + own + times(hot_ghost, returned)
            norm, curve, cross, square = reduce_all(
                [
                    column_sum(residual * residual), column_sum(direction * image),
                    column_sum(residual * image), column_sum(image * image),
                ], it
            )
            alpha = norm / curve
            solutions = solutions + alpha * direction
            residual = residual - alpha * image
            beta = (norm - 2.0 * alpha * cross + alpha * alpha * square) / norm
            direction = residual + beta * direction


def body(electroneg, hardness, tiles, pair_rows, pair_cols, pair_count, ghost_ids):
    sizes = tuple(lax.axis_size(name) for name in ("gx", "gy", "gz"))
    blocks, atoms = electroneg.shape[3:]
    pairs = tiles.shape[3]
    ghosts = ghost_ids.shape[4]
    ghost_row = jnp.pad(
        ghost_ids.reshape(1, 6 * ghosts), ((0, 0), (0, atoms - 6 * ghosts)), constant_values=-1
    )
    spreads = [sizes] if math.prod(sizes) <= DIRECT else [(sizes[0], 1, sizes[2]), (1, sizes[1], 1)]
    peers = [math.prod(spread) - 1 for spread in spreads]
    vmem = pl.BlockSpec(memory_space=pltpu.VMEM)
    wide = 2 * atoms
    dma = pltpu.SemaphoreType.DMA
    solutions, charges = pl.pallas_call(
        functools.partial(kernel, sizes, spreads, blocks, ghosts, pairs, atoms),
        out_shape=(
            jax.ShapeDtypeStruct((2, blocks, atoms), F32),
            jax.ShapeDtypeStruct((blocks, atoms), F32),
        ),
        in_specs=[pl.BlockSpec(memory_space=pltpu.SMEM)] + [vmem] * 5 + [pl.BlockSpec(memory_space=pl.ANY)],
        out_specs=(vmem, vmem),
        scratch_shapes=[
            pltpu.VMEM((pairs * atoms, atoms), F32),
            pltpu.VMEM((pairs * atoms, atoms), BF16),
            pltpu.VMEM((pairs * atoms, atoms), BF16),
            pltpu.VMEM((pairs * 4, atoms), F32),
            pltpu.VMEM((pairs * 4, atoms), F32),
            pltpu.VMEM((ITERS, 6 * ghosts, wide), F32),
            pltpu.VMEM((ITERS, 6 * ghosts, wide), F32),
            pltpu.VMEM((ITERS - 1, 6 * ghosts, wide), F32),
            pltpu.VMEM((ITERS - 1, 6 * ghosts, wide), F32),
            dma((CHUNKS,)),
            dma((ITERS, 6)), dma((ITERS, 6)),
            dma((ITERS - 1, 6)), dma((ITERS - 1, 6)),
            *[pltpu.VMEM((ITERS, 8, atoms), F32) for _ in peers],
            *[pltpu.VMEM((ITERS, n, 8, atoms), F32) for n in peers],
            *[dma((ITERS, n)) for n in peers],
            *[dma((ITERS, n)) for n in peers],
        ],
        compiler_params=pltpu.CompilerParams(
            collective_id=0, has_side_effects=True, vmem_limit_bytes=48 * 1024 * 1024
        ),
    )(
        pair_count.reshape(1, 1),
        electroneg.reshape(blocks, atoms),
        hardness.reshape(blocks, atoms),
        pair_rows.reshape(1, pairs),
        pair_cols.reshape(1, pairs),
        ghost_row,
        tiles.reshape(pairs * atoms, atoms),
    )
    return solutions.reshape((2, 1, 1, 1, blocks, atoms)), charges.reshape((1, 1, 1, blocks, atoms))


def solution(mesh):
    return jax.shard_map(
        body,
        mesh=mesh,
        in_specs=(
            P("gx", "gy", "gz", None, None),
            P("gx", "gy", "gz", None, None),
            P("gx", "gy", "gz", None, None, None),
            P("gx", "gy", "gz", None),
            P("gx", "gy", "gz", None),
            P("gx", "gy", "gz"),
            P("gx", "gy", "gz", None, None),
        ),
        out_specs=(P(None, "gx", "gy", "gz", None, None), P("gx", "gy", "gz", None, None)),
        check_vma=False,
    )
```
